512 devices in a mesh: section: 16 (over z, core), expert: 32 (over x, y).
Axes of the slice: x: 4, y: 8, z: 8, core: 2. Of those that a mesh axis runs over, the one named last changes fastest.
Arguments:
- state: bfloat16 [2, 16, 1024, 3584], P(None, 'section', 'expert'), may hold values from -6 to 6
- fresh: bfloat16 [2, 1024, 3584], P(None, 'expert'), may hold values from -6 to 6
- norm_gain: float32 [16, 3584], P('section'), may hold values from 0.5 to 1.5
- w_gate: bfloat16 [16, 3584, 4096], P('section', None, 'expert'), may hold values from -0.09375 to 0.09375
- w_up: bfloat16 [16, 3584, 4096], P('section', None, 'expert'), may hold values from -0.09375 to 0.09375
- w_down: bfloat16 [16, 4096, 3584], P('section', 'expert'), may hold values from -0.1875 to 0.1875
- routes: int32 [2, 2, 16, 1024, 2], P(None, None, 'section', 'expert'), may hold values from 0 to 3, all different within a row; in each aligned block of 32 rows (0 to 31, 32 to 63, ..., all dimensions but the last counted through in order) at most 18 rows name the same one
- gates: float32 [2, 2, 16, 1024, 2], P(None, None, 'section', 'expert'), may hold values from 0.1 to 1
Outputs:
- advanced: bfloat16 [2, 16, 1024, 3584], P(None, 'section', 'expert')
The draws below stay inside these ranges and needn't reach their ends.
Inputs may be any that keep to these rules, and one draw needn't show every extreme that they name: `routes`: each row names 2 different experts. In each aligned block of 32 rows (one device's rows of one tick, direction and section) no expert is named by more than 18 rows, and in some blocks one is named by exactly 18.
All inputs are finite; a program needn't handle non-finite values.
Results may differ from the reference program's by a relative error of at most 0.007.
Values may be sent and summed in bfloat16 or wider, within the bound.
A program may use at most 128 MiB of HBM per device.

```python
import math
import jax
import jax.numpy as jnp
import numpy as np
from jax import lax

D = 3584
HIDDEN_SIZE = 1024
EXPERTS = 4
TOP = 2
TOK_DEV = 32
CAP = 18
SECTIONS = 16
TOKENS = 1024
N_EXPERT = 32


def steps_of(rng, dims, shards, least, largest):
    gain = 1.0
    for axis_at, blocks in shards:
        steps = jax.random.uniform(jax.random.fold_in(jax.random.fold_in(rng, 6), axis_at), (blocks,), jnp.float32, least / len(shards), largest / len(shards))
        gain = gain * jnp.repeat(jnp.exp(steps), dims[axis_at] // blocks).reshape((-1,) + (1,) * (len(dims) - 1 - axis_at))
    return gain


def deal_out(stream_key, own, number, rows, amount, top, reach, slope):
    sequence = jax.random.permutation(stream_key, amount)
    packed, common = load_shares(amount, rows * top, reach, slope, True), load_shares(amount, rows * top, reach, slope, False)
    places = jnp.arange(amount)

    def named(sizes, rotation):
        used = int((sizes > 0).sum())
        fixed = max(1, used // 4)
        moved = fixed + (places - fixed + rotation * (used - fixed)) % max(1, amount - fixed)
        return jnp.zeros((amount,), jnp.int32).at[sequence[jnp.where(places < fixed, places, moved)]].set(jnp.asarray(sizes, jnp.int32))

    sizes = jnp.where(number % 4 == 0, named(packed, number // 4), named(common, number - number // 4 - 1))
    mixed = jax.random.permutation(jax.random.fold_in(own, 3), amount)
    giver, taker = mixed[0:amount // 2 * 2:2], mixed[1:amount // 2 * 2:2]
    room = jnp.minimum(sizes[giver] - 1, reach - sizes[taker]) // 2
    room = jnp.where((giver == sequence[0]) | (taker == sequence[0]) | (sizes[taker] == 0), 0, jnp.maximum(room, 0))
    moved = jax.random.randint(jax.random.fold_in(own, 4), (amount // 2,), 0, 1 << 20) % (room + 1)
    sizes = sizes.at[giver].add(-moved).at[taker].add(moved)
    members = jnp.searchsorted(jnp.cumsum(sizes), jnp.arange(rows * top), side="right").astype(jnp.int32)
    table = members.reshape(top, rows).T
    table = table[jax.random.permutation(jax.random.fold_in(own, 1), rows)]
    rotation = jax.random.randint(jax.random.fold_in(own, 2), (rows, 1), 0, top)
    return jnp.take_along_axis(table, (jnp.arange(top)[None, :] + rotation) % top, axis=1)


def load_shares(number_of, total, most, skew, full):
    portions = [(1 << 20) // math.isqrt(standing ** skew) + 1 for standing in range(1, number_of + 1)]
    largest = most if full else min(most, max(-(-total // number_of), total * portions[0] // sum(portions)))
    least = 1 if total - largest >= number_of - 1 else 0
    given, spare = [largest] + [least] * (number_of - 1), total - largest - least * (number_of - 1)
    while spare > 0:
        movable = [i for i in range(1, number_of) if given[i] < largest] or [i for i in range(1, number_of) if given[i] < most]
        mass, left = sum([portions[i] for i in movable]), spare
        for i in movable:
            addition = min(most - given[i], max(1, left * portions[i] // mass), spare)
            given[i] = given[i] + addition
            spare = spare - addition
    return np.array(given)


def scatter_about(key, dims, deviation, bound, cuts=(), held_as=jnp.bfloat16):
    factor_of = steps_of(key, dims, cuts, -0.22, 0.18) if cuts else 1.0
    array = jax.random.normal(key, dims, jnp.float32) * deviation * factor_of
    return jnp.minimum(jnp.maximum(array, -bound), bound).astype(held_as)


def setup_inputs(seed: int = 0) -> dict:
    splits = jax.random.split(jax.random.key(seed), 9)
    state = scatter_about(splits[0], (2, SECTIONS, TOKENS, D), 1.0, 6.0, ((1, 16), (2, 32)))
    fresh = scatter_about(splits[1], (2, TOKENS, D), 1.0, 6.0, ((1, 32),))
    norm_gain = jnp.clip(0.5 + 1.0 * jax.random.uniform(splits[2], (SECTIONS, D), jnp.float32) ** steps_of(splits[2], (SECTIONS, D), ((0, 16),), -0.2, 0.2), 0.5, 1.5)
    w_gate = scatter_about(splits[3], (SECTIONS, D, EXPERTS * HIDDEN_SIZE), D ** -0.5, 0.09375, ((0, 16), (2, 32)))
    w_up = scatter_about(splits[4], (SECTIONS, D, EXPERTS * HIDDEN_SIZE), D ** -0.5, 0.09375, ((0, 16), (2, 32)))
    w_down = scatter_about(splits[5], (SECTIONS, EXPERTS * HIDDEN_SIZE, D), HIDDEN_SIZE ** -0.5, 0.1875, ((0, 16), (1, 32)))
    routes_keys = jax.random.split(jax.random.fold_in(splits[6], 1), 2 * 2 * SECTIONS * TOKENS // TOK_DEV)
    routes_turns = jax.random.permutation(jax.random.fold_in(splits[6], 3), 2 * 2 * SECTIONS * TOKENS // TOK_DEV)
    routes = jax.vmap(lambda own, number: deal_out(jax.random.fold_in(splits[6], 2), own, number, TOK_DEV, EXPERTS, TOP, CAP, 2))(routes_keys, routes_turns).reshape((2, 2, SECTIONS, TOKENS, TOP))
    gates = jnp.clip(0.1 + 0.9 * jax.random.uniform(splits[7], (2, 2, SECTIONS, TOKENS, TOP), jnp.float32) ** steps_of(splits[7], (2, 2, SECTIONS, TOKENS, TOP), ((2, 16), (3, 32)), -0.2, 0.2), 0.1, 1.0)
    return {"state": state, "fresh": fresh, "norm_gain": norm_gain, "w_gate": w_gate, "w_up": w_up, "w_down": w_down, "routes": routes, "gates": gates}


def build_slots(route_ids):
    is_hit = jnp.any(route_ids[..., None] == jnp.arange(EXPERTS, dtype=jnp.int32), axis=-2)
    slot_rank = jnp.cumsum(is_hit.astype(jnp.int32), axis=-2) - 1
    return is_hit[..., None] & (slot_rank[..., None] == jnp.arange(CAP, dtype=jnp.int32))

def moe_layer(x_rows, route_ids, route_wts, norm_scale, gate_w, up_w, down_w):
    group_size = N_EXPERT // EXPERTS
    hid_dev = HIDDEN_SIZE // group_size
    x_wide = x_rows.astype(jnp.float32)
    mean_sq = lax.optimization_barrier(jnp.mean(x_wide * x_wide, axis=-1, keepdims=True))
    normed = (x_wide * lax.rsqrt(mean_sq + 1e-06) * norm_scale).astype(jnp.bfloat16)
    block_ids = route_ids.reshape(N_EXPERT, TOK_DEV, TOP)
    block_wts = route_wts.reshape(N_EXPERT, TOK_DEV, TOP)
    slot_map = build_slots(block_ids)
    token_ids = jnp.arange(TOKENS, dtype=jnp.int32).reshape(N_EXPERT, TOK_DEV)
    slot_token = lax.optimization_barrier(jnp.sum(jnp.where(slot_map, token_ids[:, :, None, None], 0), axis=1)).astype(jnp.int32)
    expert_hit = block_ids[..., None] == jnp.arange(EXPERTS, dtype=jnp.int32)
    weight = lax.optimization_barrier(jnp.sum(jnp.where(expert_hit, block_wts[..., None], jnp.float32(0.0)), axis=2))
    outputs = []
    for expert_idx in range(EXPERTS):
        picked = slot_token[:, expert_idx, :].reshape(-1)
        slot_rows = normed[picked]
        lower = expert_idx * HIDDEN_SIZE
        gate_out = jnp.dot(slot_rows, gate_w[:, lower:lower + HIDDEN_SIZE], preferred_element_type=jnp.float32)
        up_out = jnp.dot(slot_rows, up_w[:, lower:lower + HIDDEN_SIZE], preferred_element_type=jnp.float32)
        hidden = (jax.nn.silu(gate_out) * up_out).astype(jnp.bfloat16)
        hid_split = hidden.reshape(-1, group_size, hid_dev).astype(jnp.float32)
        down_split = down_w[lower:lower + HIDDEN_SIZE].reshape(group_size, hid_dev, -1).astype(jnp.float32)
        partials = jnp.einsum('rgh,ghd->grd', hid_split, down_split, precision=lax.Precision.HIGHEST)
        partials = lax.optimization_barrier(partials.astype(jnp.bfloat16)).astype(jnp.float32)
        outputs.append(lax.optimization_barrier(jnp.sum(partials, axis=0)).reshape(N_EXPERT, CAP, -1))
    expert_out = jnp.stack(outputs, axis=1)
    combine_wt = slot_map.astype(jnp.float32) * weight[..., None]
    mixed_sum = jnp.einsum('bnec,becd->bnd', combine_wt, expert_out, precision=lax.Precision.HIGHEST)
    return (x_wide + mixed_sum.reshape(TOKENS, -1)).astype(jnp.bfloat16)

def reference(state, fresh, norm_gain, w_gate, w_up, w_down, routes, gates):

    def section_layers(tick_idx, direction, inputs):

        def per_section(section_args):
            return moe_layer(*section_args)
        return lax.map(per_section, (inputs, routes[tick_idx, direction], gates[tick_idx, direction], norm_gain, w_gate, w_up, w_down))
    first_fwd = section_layers(0, 0, state[0])
    first_rev = section_layers(0, 1, state[1])
    input_fwd = jnp.concatenate([fresh[0][None], first_fwd[:-1]], axis=0)
    input_rev = jnp.concatenate([first_rev[1:], fresh[1][None]], axis=0)
    return jnp.stack([section_layers(1, 0, input_fwd), section_layers(1, 1, input_rev)], axis=0)
```

```python
import functools

import jax
import jax.numpy as jnp
from jax import lax
from jax.experimental import pallas as pl
from jax.experimental.pallas import tpu as pltpu
from jax.sharding import PartitionSpec as P

MESH = pl.DeviceIdType.MESH
NX, NY = 4, 8
ROWS = 32
HALF = ROWS // 2
D = 3584
HID = 128
NC = 4
COLS = D // NC
NQ = 4
QROWS = D // NQ
N_SEMS = 240
F32, BF16 = jnp.float32, jnp.bfloat16


def kernel(n_section, state, fresh, gain, w_gate, w_up, w_down, routes, gates, out,
           wgu, wd, xn, hid, part, rsb, snd, xs, xin, cw, send_sem, recv_sem, local_sem):
    expert = lax.axis_index("expert")
    section = lax.axis_index("section")
    ix, iy = expert // NY, expert % NY

    def along(dx, dy):
        return {"expert": ((ix + dx + NX) % NX) * NY + (iy + dy + NY) % NY}

    right, left = along(0, 1), along(0, -1)
    x_right, x_left = along(1, 0), along(-1, 0)
    onward = {"section": (section + 1) % n_section}
    backward = {"section": (section + n_section - 1) % n_section}

    count = [0]
    sent = []

    def copy_to(src, dst, device):
        at = count[0]
        count[0] += 1
        copy = pltpu.make_async_remote_copy(
            src_ref=src, dst_ref=dst, send_sem=send_sem.at[at], recv_sem=recv_sem.at[at],
            device_id=device, device_id_type=MESH)
        sent.append(copy)
        return copy

    barrier = pltpu.get_barrier_semaphore()
    for peer in (right, left, x_right, x_left, onward, backward):
        pl.semaphore_signal(barrier, inc=1, device_id=peer, device_id_type=MESH)

    own = []
    for q in range(NQ):
        rows = pl.ds(q * QROWS, QROWS)
        own.append((
            pltpu.make_async_copy(w_gate.at[0, rows], wgu.at[0, rows, pl.ds(0, HID)], local_sem.at[2 * q]),
            pltpu.make_async_copy(w_up.at[0, rows], wgu.at[0, rows, pl.ds(HID, HID)], local_sem.at[2 * q + 1])))
    own_wd = pltpu.make_async_copy(w_down.at[0], wd.at[pl.ds(0, HID)], local_sem.at[2 * NQ])
    for q in (0, 2, 1, 3):
        own[q][0].start()
        own[q][1].start()
    own_wd.start()

    def normed(x):
        wide = x.astype(F32)
        mean_sq = jnp.mean(wide * wide, axis=-1, keepdims=True)
        return (wide * lax.rsqrt(mean_sq + 1e-06) * gain[...]).astype(BF16)

    def slot(s, half=None):
        if half is None:
            return pl.ds(s * ROWS, ROWS)
        return pl.ds(s * ROWS + half * HALF, HALF)

    for d in range(2):
        xn[0, d, slot(0)] = normed(state[d, 0])

    column_expert = (ix + NX - lax.broadcasted_iota(jnp.int32, (ROWS, 128), 1) % NX) % NX
    for t in range(2):
        for d in range(2):
            ids, wts = routes[t, d, 0], gates[t, d, 0]
            cw[0, pl.ds((t * 2 + d) * ROWS, ROWS)] = (
                jnp.where(ids[:, 0:1] == column_expert, wts[:, 0:1], 0.0)
                + jnp.where(ids[:, 1:2] == column_expert, wts[:, 1:2], 0.0))

    pl.semaphore_wait(barrier, 6)

    def q_rows(q):
        return pl.ds(q * QROWS, QROWS)

    gu_r = [copy_to(wgu.at[0, q_rows(q)], wgu.at[1, q_rows(q)], x_right) for q in range(NQ)]
    gu_l = [copy_to(wgu.at[0, q_rows(q)], wgu.at[3, q_rows(q)], x_left) for q in range(NQ)]
    gu_fr = {q: copy_to(wgu.at[1, q_rows(q)], wgu.at[2, q_rows(q)], x_right) for q in (0, 1)}
    gu_fl = {q: copy_to(wgu.at[3, q_rows(q)], wgu.at[2, q_rows(q)], x_left) for q in (2, 3)}

    def cols(c):
        return pl.ds(c * COLS, COLS)

    def wd_at(r, c, half=None):
        if half is None:
            return wd.at[pl.ds(r * HID, HID), cols(c)]
        return wd.at[pl.ds(r * HID + half * (HID // 2), HID // 2), cols(c)]

    wd_r = [copy_to(wd_at(0, c), wd_at(1, c), x_right) for c in range(NC)]
    wd_l = [copy_to(wd_at(0, c), wd_at(3, c), x_left) for c in range(NC)]
    wd_fr = [copy_to(wd_at(1, c, 0), wd_at(2, c, 0), x_right) for c in range(NC)]
    wd_fl = [copy_to(wd_at(3, c, 1), wd_at(2, c, 1), x_left) for c in range(NC)]

    def gather(t, d):
        ring = []
        for h in range(4):
            a, b = (0, 1) if h == 3 else (None, None)
            ring.append((
                copy_to(xn.at[t, d, slot(h, a)], xn.at[t, d, slot(h + 1, a)], right),
                copy_to(xn.at[t, d, slot((8 - h) % 8, b)], xn.at[t, d, slot(7 - h, b)], left)))
        return ring

    ag = [[gather(t, d) for d in range(2)] for t in range(2)]

    def ag_hop(t, d, h):
        for side in range(2):
            if h > 0:
                ag[t][d][h - 1][side].wait_recv()
            if h < 4:
                ag[t][d][h][side].start()

    cw_ring = [(copy_to(cw.at[h], cw.at[h + 1], right),
                copy_to(cw.at[(8 - h) % 8], cw.at[7 - h], left) if h < 3 else None) for h in range(4)]

    def gate_up(t, d, r):
        joined = jnp.dot(xn[t, d], wgu[r], preferred_element_type=F32)
        g, u = joined[:, :HID], joined[:, HID:]
        weights = cw[:, pl.ds(pl.multiple_of((t * 2 + d) * ROWS, ROWS), ROWS), :].reshape(NY * ROWS, 128)
        lane = lax.broadcasted_iota(jnp.int32, weights.shape, 1)
        weight = jnp.sum(jnp.where(lane == r, weights, 0.0), axis=1, keepdims=True)
        hidden = g / (1.0 + jnp.exp(-g)) * u * weight
        hid[d, :, pl.ds(pl.multiple_of(r * HID, HID), HID)] = hidden.astype(BF16)

    def down(d, c):
        part[d, :, cols(c)] = jnp.dot(hid[d], wd[:, cols(c)], preferred_element_type=F32)

    def scatter(t, d, c):
        ring = []
        for h in range(4):
            if h == 0:
                ring.append((
                    copy_to(snd.at[t, d, pl.ds(0, HALF), cols(c)], rsb.at[t, d, 0, 0, pl.ds(0, HALF), cols(c)], right),
                    copy_to(snd.at[t, d, pl.ds(HALF, HALF), cols(c)], rsb.at[t, d, 1, 0, pl.ds(HALF, HALF), cols(c)], left)))
            else:
                ring.append((
                    copy_to(rsb.at[t, d, 0, h - 1, :, cols(c)], rsb.at[t, d, 0, h, :, cols(c)], right),
                    copy_to(rsb.at[t, d, 1, h - 1, :, cols(c)], rsb.at[t, d, 1, h, :, cols(c)], left)))
        return ring

    rs = [[[scatter(t, d, c) for c in range(NC)] for d in range(2)] for t in range(2)]

    def rs_hop(t, d, c, h):
        ring = rs[t][d][c]
        if h == 0:
            snd[t, d, :, cols(c)] = part[d, slot(4), cols(c)].astype(BF16)
            ring[0][0].start()
            ring[0][1].start()
            return
        for side in range(2):
            mine = (4 + h) if side == 0 else (4 - h)
            ring[h - 1][side].wait_recv()
            buf = rsb.at[t, d, side, h - 1]
            if h == 1:
                both, lone = (0, 1) if side == 0 else (1, 0)
                at = pl.ds(both * HALF, HALF)
                buf[at, cols(c)] = (buf[at, cols(c)].astype(F32) + part[d, slot(mine, both), cols(c)]).astype(BF16)
                buf[pl.ds(lone * HALF, HALF), cols(c)] = part[d, slot(mine, lone), cols(c)].astype(BF16)
            else:
                buf[:, cols(c)] = (buf[:, cols(c)].astype(F32) + part[d, slot(mine), cols(c)]).astype(BF16)
            ring[h][side].start()

    def rs_sum(t, d, c, x):
        rs[t][d][c][3][0].wait_recv()
        rs[t][d][c][3][1].wait_recv()
        mixed = (part[d, slot(0), cols(c)] + rsb[t, d, 0, 3, :, cols(c)].astype(F32)
                 + rsb[t, d, 1, 3, :, cols(c)].astype(F32))
        return (x.astype(F32) + mixed).astype(BF16)

    shift = [[copy_to(xs.at[d, :, cols(c)], xin.at[d, :, cols(c)], onward if d == 0 else backward)
              for c in range(NC)] for d in range(2)]

    def hand_on(d, c):
        xs[d, :, cols(c)] = rs_sum(0, d, c, state[d, 0, :, cols(c)])
        shift[d][c].start()

    def next_input(d):
        for c in range(NC):
            shift[d][c].wait_recv()

        @pl.when(section == (0 if d == 0 else n_section - 1))
        def _():
            xin[d] = fresh[d]

        xn[1, d, slot(0)] = normed(xin[d])

    def own_ready(q):
        own[q][0].wait()
        own[q][1].wait()

    for q in (0, 2, 1, 3):
        own_ready(q)
    gu_r[0].start()
    gu_l[2].start()
    ag_hop(0, 0, 0)
    ag_hop(0, 1, 0)
    gu_r[1].start()
    gu_l[3].start()
    own_wd.wait()
    ag_hop(0, 0, 1)
    ag_hop(0, 1, 1)
    gu_r[2].start()
    gu_l[0].start()
    ag_hop(0, 0, 2)
    ag_hop(0, 1, 2)
    gu_r[3].start()
    gu_l[1].start()
    ag_hop(0, 0, 3)
    ag_hop(0, 1, 3)
    cw_ring[0][0].start()
    cw_ring[0][1].start()
    gu_r[0].wait_recv()
    gu_fr[0].start()
    gu_l[2].wait_recv()
    gu_fl[2].start()
    ag_hop(0, 0, 4)
    ag_hop(0, 1, 4)
    for h in range(1, 5):
        for side in range(2):
            if cw_ring[h - 1][side] is not None:
                cw_ring[h - 1][side].wait_recv()
            if h < 4 and cw_ring[h][side] is not None:
                cw_ring[h][side].start()
    gu_r[1].wait_recv()
    gu_fr[1].start()
    gu_l[3].wait_recv()
    gu_fl[3].start()
    for c in (0, 1):
        wd_r[c].start()
        wd_l[c].start()

    def both(r):
        @pl.loop(0, 2)
        def _(d):
            gate_up(0, d, r)

    both(0)
    gu_r[2].wait_recv()
    gu_r[3].wait_recv()
    both(1)
    gu_l[0].wait_recv()
    gu_l[1].wait_recv()
    both(3)
    gu_fr[0].wait_recv()
    gu_fl[2].wait_recv()
    gu_fr[1].wait_recv()
    gu_fl[3].wait_recv()
    for c in (2, 3):
        wd_r[c].start()
        wd_l[c].start()
    wd_r[0].wait_recv()
    wd_fr[0].start()
    wd_l[0].wait_recv()
    wd_fl[0].start()
    both(2)

    for phase in range(2 * NC + 4):
        i, odd = phase // 2, phase % 2
        if odd == 0:
            if i < NC:
                if i + 1 < NC:
                    wd_r[i + 1].wait_recv()
                    wd_fr[i + 1].start()
                    wd_l[i + 1].wait_recv()
                    wd_fl[i + 1].start()
                wd_fr[i].wait_recv()
                wd_fl[i].wait_recv()
            for d in range(2):
                if 0 <= i - 2 < NC:
                    hand_on(d, i - 2)
                if 0 <= i - 1 < NC:
                    rs_hop(0, d, i - 1, 2)
                if i < NC:
                    down(d, i)
                    rs_hop(0, d, i, 0)
        else:
            for d in range(2):
                if 0 <= i - 1 < NC:
                    rs_hop(0, d, i - 1, 3)
                if i < NC:
                    rs_hop(0, d, i, 1)

    for d in range(2):
        next_input(d)
        ag_hop(1, d, 0)
    for h in range(1, 4):
        ag_hop(1, 0, h)
        ag_hop(1, 1, h)

    def experts(d):
        @pl.loop(0, NX)
        def _(r):
            gate_up(1, d, r)

    ag_hop(1, 0, 4)
    experts(0)
    for c in range(NC):
        down(0, c)
        rs_hop(1, 0, c, 0)
    ag_hop(1, 1, 4)
    for c in range(NC):
        rs_hop(1, 0, c, 1)
    experts(1)
    for c in range(NC):
        rs_hop(1, 0, c, 2)
    for c in range(NC):
        down(1, c)
        rs_hop(1, 1, c, 0)
    for c in range(NC):
        rs_hop(1, 0, c, 3)
    for c in range(NC):
        rs_hop(1, 1, c, 1)
    for c in range(NC):
        out[0, 0, :, cols(c)] = rs_sum(1, 0, c, xin[0, :, cols(c)])
    for h in (2, 3):
        for c in range(NC):
            rs_hop(1, 1, c, h)
    for c in range(NC):
        out[1, 0, :, cols(c)] = rs_sum(1, 1, c, xin[1, :, cols(c)])

    for copy in sent:
        copy.wait_send()


def solution(mesh):
    n_section = mesh.shape["section"]

    def per_device(state, fresh, norm_gain, w_gate, w_up, w_down, routes, gates):
        vmem = pl.BlockSpec(memory_space=pltpu.VMEM)
        hbm = pl.BlockSpec(memory_space=pl.ANY)
        return pl.pallas_call(
            functools.partial(kernel, n_section),
            out_shape=jax.ShapeDtypeStruct(state.shape, state.dtype),
            in_specs=[vmem, vmem, vmem, hbm, hbm, hbm, vmem, vmem],
            out_specs=vmem,
            scratch_shapes=[
                pltpu.VMEM((NX, D, 2 * HID), BF16),
                pltpu.VMEM((NX * HID, D), BF16),
                pltpu.VMEM((2, 2, NY * ROWS, D), BF16),
                pltpu.VMEM((2, NY * ROWS, NX * HID), BF16),
                pltpu.VMEM((2, NY * ROWS, D), F32),
                pltpu.VMEM((2, 2, 2, 4, ROWS, D), BF16),
                pltpu.VMEM((2, 2, ROWS, D), BF16),
                pltpu.VMEM((2, ROWS, D), BF16),
                pltpu.VMEM((2, ROWS, D), BF16),
                pltpu.VMEM((NY, 4 * ROWS, 128), F32),
                pltpu.SemaphoreType.DMA((N_SEMS,)),
                pltpu.SemaphoreType.DMA((N_SEMS,)),
                pltpu.SemaphoreType.DMA((2 * NQ + 1,)),
            ],
            compiler_params=pltpu.CompilerParams(
                collective_id=0, has_side_effects=True, vmem_limit_bytes=58 * 2**20),
        )(state, fresh, norm_gain, w_gate, w_up, w_down, routes, gates)

    rows = P(None, "section", "expert", None)
    named = P(None, None, "section", "expert", None)
    return jax.shard_map(
        per_device, mesh=mesh,
        in_specs=(rows, P(None, "expert", None), P("section", None), P("section", None, "expert"),
                  P("section", None, "expert"), P("section", "expert", None), named, named),
        out_specs=rows, check_vma=False)
```

```python
import functools

import jax
import jax.numpy as jnp
from jax import lax
from jax.experimental import pallas as pl
from jax.experimental.pallas import tpu as pltpu
from jax.sharding import PartitionSpec as P

MESH = pl.DeviceIdType.MESH
NX, NY = 4, 8
ROWS = 32
HALF = ROWS // 2
D = 3584
HID = 128
NC = (7, 4)
COLS = (D // NC[0], D // NC[1])
QROWS = D // 2
N_SEMS = 320
F32, BF16 = jnp.float32, jnp.bfloat16


def kernel(n_section, state, fresh, gain, w_gate, w_up, w_down, routes, gates, out,
           wgu, wd, xn, hid, part, rsb, snd, xs, xin, cw, send_sem, recv_sem, local_sem):
    expert = lax.axis_index("expert")
    section = lax.axis_index("section")
    ix, iy = expert // NY, expert % NY

    def along(dx, dy):
        return {"expert": ((ix + dx + NX) % NX) * NY + (iy + dy + NY) % NY}

    right, left = along(0, 1), along(0, -1)
    x_right, x_left = along(1, 0), along(-1, 0)
    onward = {"section": (section + 1) % n_section}
    backward = {"section": (section + n_section - 1) % n_section}

    count = [0]
    sent = []

    def reserve(n):
        count[0] += n
        return count[0] - n

    def copy_to(src, dst, device, at=None):
        keep = at is None
        if keep:
            at = reserve(1)
        copy = pltpu.make_async_remote_copy(
            src_ref=src, dst_ref=dst, send_sem=send_sem.at[at], recv_sem=recv_sem.at[at],
            device_id=device, device_id_type=MESH)
        if keep:
            sent.append(copy)
        return copy

    barrier = pltpu.get_barrier_semaphore()
    for peer in (right, left, x_right, x_left, onward, backward):
        pl.semaphore_signal(barrier, inc=1, device_id=peer, device_id_type=MESH)

    own = [
        pltpu.make_async_copy(w_gate.at[0], wgu.at[0, :, pl.ds(0, HID)], local_sem.at[0]),
        pltpu.make_async_copy(w_up.at[0], wgu.at[0, :, pl.ds(HID, HID)], local_sem.at[1]),
        pltpu.make_async_copy(w_down.at[0], wd.at[pl.ds(0, HID)], local_sem.at[2])]

    def normed(x):
        wide = x.astype(F32)
        mean_sq = jnp.mean(wide * wide, axis=-1, keepdims=True)
        return (wide * lax.rsqrt(mean_sq + 1e-06) * gain[...]).astype(BF16)

    def slot(s, half=None):
        if half is None:
            return pl.ds(s * ROWS, ROWS)
        return pl.ds(s * ROWS + half * HALF, HALF)

    def q_rows(q):
        return pl.ds(q * QROWS, QROWS)

    def gu_own(q, r, device):
        return [copy_to(w.at[0, q_rows(q)], wgu.at[r, q_rows(q), pl.ds(k * HID, HID)], device)
                for k, w in enumerate((w_gate, w_up))]

    gu_r = [gu_own(q, 1, x_right) for q in range(2)]
    gu_l = [gu_own(q, 3, x_left) for q in range(2)]
    gu_fr = copy_to(wgu.at[1, q_rows(0)], wgu.at[2, q_rows(0)], x_right)
    gu_fl = copy_to(wgu.at[3, q_rows(1)], wgu.at[2, q_rows(1)], x_left)

    def cols(t, c):
        at = c * COLS[t]
        return pl.ds(at if isinstance(c, int) else pl.multiple_of(at, 128), COLS[t])

    def wd_at(r, c, half=None):
        if half is None:
            return wd.at[pl.ds(r * HID, HID), cols(0, c)]
        return wd.at[pl.ds(r * HID + half * (HID // 2), HID // 2), cols(0, c)]

    wd_sems = reserve(4 * NC[0])

    def wd_own(c):
        return (copy_to(w_down.at[0, :, cols(0, c)], wd_at(1, c), x_right, wd_sems + 4 * c),
                copy_to(w_down.at[0, :, cols(0, c)], wd_at(3, c), x_left, wd_sems + 4 * c + 1))

    def wd_on(c):
        return (copy_to(wd_at(1, c, 0), wd_at(2, c, 0), x_right, wd_sems + 4 * c + 2),
                copy_to(wd_at(3, c, 1), wd_at(2, c, 1), x_left, wd_sems + 4 * c + 3))

    def wd_pass(c):
        for came, on in zip(wd_own(c), wd_on(c)):
            came.wait_recv()
            on.start()

    def start(copies):
        for copy in copies:
            copy.start()

    def arrive(copies):
        for copy in copies:
            copy.wait_recv()

    def gather(t, d):
        ring = []
        for h in range(4):
            pieces = []
            for k in range(2):
                to_right = to_left = None
                if h < 3 or k == 0:
                    to_right = copy_to(xn.at[t, d, slot(h, k)], xn.at[t, d, slot(h + 1, k)], right)
                if h < 3 or k == 1:
                    to_left = copy_to(xn.at[t, d, slot((8 - h) % 8, k)], xn.at[t, d, slot(7 - h, k)], left)
                pieces.append((to_right, to_left))
            ring.append(pieces)
        return ring

    ag = [[gather(t, d) for d in range(2)] for t in range(2)]

    def ag_hop(t, d, h):
        for k in range(2):
            for side in range(2):
                if h > 0 and ag[t][d][h - 1][k][side] is not None:
                    ag[t][d][h - 1][k][side].wait_recv()
                if h < 4 and ag[t][d][h][k][side] is not None:
                    ag[t][d][h][k][side].start()

    cw_ring = [(copy_to(cw.at[h], cw.at[h + 1], right),
                copy_to(cw.at[(8 - h) % 8], cw.at[7 - h], left) if h < 3 else None) for h in range(4)]

    def cw_hop(h):
        for side in range(2):
            if h > 0 and cw_ring[h - 1][side] is not None:
                cw_ring[h - 1][side].wait_recv()
            if h < 4 and cw_ring[h][side] is not None:
                cw_ring[h][side].start()

    def combine_weights():
        column_expert = ((ix + NX - lax.broadcasted_iota(jnp.int32, (ROWS, 128), 1) % NX) % NX).astype(F32)
        eye = (lax.broadcasted_iota(jnp.int32, (ROWS, ROWS), 0)
               == lax.broadcasted_iota(jnp.int32, (ROWS, ROWS), 1))

        def column(row):
            return jnp.sum(jnp.where(eye, row, 0.0), axis=1, keepdims=True)

        for t in range(2):
            for d in range(2):
                ids, wts = routes[t, d, 0].astype(F32), gates[t, d, 0]
                cw[0, pl.ds((t * 2 + d) * ROWS, ROWS)] = (
                    jnp.where(column(ids[0:1]) == column_expert, column(wts[0:1]), 0.0)
                    + jnp.where(column(ids[1:2]) == column_expert, column(wts[1:2]), 0.0))

    def gate_up(t, d, r, first=0, last=NY):
        rows = pl.ds(first * ROWS, (last - first) * ROWS)
        joined = jnp.dot(xn[t, d, rows], wgu[r], preferred_element_type=F32)
        g, u = joined[:, :HID], joined[:, HID:]
        own_rows = pl.ds(pl.multiple_of((t * 2 + d) * ROWS, ROWS), ROWS)
        weights = cw[first:last, own_rows, :].reshape((last - first) * ROWS, 128)
        lane = lax.broadcasted_iota(jnp.int32, weights.shape, 1)
        weight = jnp.sum(jnp.where(lane == r, weights, 0.0), axis=1, keepdims=True)
        hidden = g / (1.0 + jnp.exp(-g)) * u * weight
        hid[d, rows, pl.ds(pl.multiple_of(r * HID, HID), HID)] = hidden.astype(BF16)

    def down(d, at):
        part[d, :, at] = jnp.dot(hid[d], wd[:, at], preferred_element_type=F32)

    rs_sems = [reserve(16 * n) for n in NC]

    def rs_copies(t, d, c, h):
        at = rs_sems[t] + ((d * NC[t] + c) * 4 + h) * 2
        if h == 0:
            return [copy_to(snd.at[t, d, pl.ds(k * HALF, HALF), cols(t, c)],
                            rsb.at[t, k, 0, d, pl.ds(k * HALF, HALF), cols(t, c)], (right, left)[k], at + k)
                    for k in range(2)]
        return [copy_to(rsb.at[t, k, h - 1, d, :, cols(t, c)], rsb.at[t, k, h, d, :, cols(t, c)],
                        (right, left)[k], at + k) for k in range(2)]

    def rs_hop(t, d, c, h):
        at_cols, onto = cols(t, c), rs_copies(t, d, c, h)
        if h == 0:
            snd[t, d, :, at_cols] = part[d, slot(4), at_cols].astype(BF16)
            start(onto)
            return
        came = rs_copies(t, d, c, h - 1)
        for side in range(2):
            mine = (4 + h) if side == 0 else (4 - h)
            came[side].wait_recv()
            buf = rsb.at[t, side, h - 1, d]
            if h == 1:
                at, lone = pl.ds(side * HALF, HALF), pl.ds((1 - side) * HALF, HALF)
                buf[at, at_cols] = (buf[at, at_cols].astype(F32) + part[d, slot(mine, side), at_cols]).astype(BF16)
                buf[lone, at_cols] = part[d, slot(mine, 1 - side), at_cols].astype(BF16)
            else:
                buf[:, at_cols] = (buf[:, at_cols].astype(F32) + part[d, slot(mine), at_cols]).astype(BF16)
            onto[side].start()

    def rs_sum(t, d, c, x):
        at_cols = cols(t, c)
        arrive(rs_copies(t, d, c, 3))
        mixed = (part[d, slot(0), at_cols] + rsb[t, 0, 3, d, :, at_cols].astype(F32)
                 + rsb[t, 1, 3, d, :, at_cols].astype(F32))
        return (x.astype(F32) + mixed).astype(BF16)

    shift_sems = reserve(2 * NC[0])

    def shift(d, c):
        return copy_to(xs.at[d, :, cols(0, c)], xin.at[d, :, cols(0, c)], {"section": (
            section + n_section + 1 - 2 * d) % n_section}, shift_sems + d * NC[0] + c)

    def hand_on(d, c):
        xs[d, :, cols(0, c)] = rs_sum(0, d, c, state[d, 0, :, cols(0, c)])
        shift(d, c).start()

    def next_input(d):
        for c in range(NC[0]):
            shift(d, c).wait_recv()

        @pl.when(section == (0 if d == 0 else n_section - 1))
        def _():
            xin[d] = fresh[d]

        xn[1, d, slot(0)] = normed(xin[d])

    pl.semaphore_wait(barrier, 6)
    start(gu_r[0])
    start(gu_l[1])
    start(gu_r[1])
    start(gu_l[0])
    for copy in own:
        copy.start()
    xn[0, 0, slot(0)] = normed(state[0, 0])
    ag_hop(0, 0, 0)
    xn[0, 1, slot(0)] = normed(state[1, 0])
    ag_hop(0, 1, 0)
    combine_weights()
    cw_hop(0)
    ag_hop(0, 0, 1)
    ag_hop(0, 1, 1)
    cw_hop(1)
    arrive(gu_r[0])
    gu_fr.start()
    arrive(gu_l[1])
    gu_fl.start()
    ag_hop(0, 0, 2)
    ag_hop(0, 1, 2)
    for c in (0, 1):
        start(wd_own(c))
    cw_hop(2)
    ag_hop(0, 0, 3)
    ag_hop(0, 1, 3)
    cw_hop(3)
    ag_hop(0, 0, 4)
    ag_hop(0, 1, 4)
    cw_hop(4)
    for copy in own:
        copy.wait()
    arrive(gu_r[1])
    arrive(gu_l[0])

    @pl.loop(0, 6)
    def _(j):
        gate_up(0, j % 2, j // 2 + j // 4)

    gu_fr.wait_recv()
    gu_fl.wait_recv()

    @pl.loop(0, 2)
    def _(d):
        gate_up(0, d, 2)

    wd_pass(0)
    start(wd_own(2))

    def back_hops(d, i):
        for h in (4, 3, 2, 1):
            if 0 <= i - h < NC[0]:
                if h == 4:
                    hand_on(d, i - h)
                else:
                    rs_hop(0, d, i - h, h)

    for i in range(NC[0] + 4):
        back_hops(0, i)
        if i + 1 < NC[0]:
            wd_pass(i + 1)
        if i + 3 < NC[0]:
            start(wd_own(i + 3))
        if i < NC[0]:
            arrive(wd_on(i))

            @pl.loop(0, 2)
            def _(d):
                down(d, cols(0, i))

            rs_hop(0, 0, i, 0)
        back_hops(1, i - 2)
        if 0 <= i - 2 < NC[0]:
            rs_hop(0, 1, i - 2, 0)

    back_hops(1, NC[0] + 2)
    next_input(0)
    ag_hop(1, 0, 0)
    back_hops(1, NC[0] + 3)
    ag_hop(1, 0, 1)
    next_input(1)
    ag_hop(1, 1, 0)
    ag_hop(1, 0, 2)
    ag_hop(1, 1, 1)
    ag_hop(1, 0, 3)

    def experts(d, half):
        @pl.loop(0, NX)
        def _(r):
            gate_up(1, d, r, half * NY // 2, (half + 1) * NY // 2)

    def all_down(d):
        @pl.loop(0, D // 512)
        def _(c):
            down(d, pl.ds(pl.multiple_of(c * 512, 512), 512))

    def hop_all(d, h):
        for c in range(NC[1]):
            if h < 4:
                rs_hop(1, d, c, h)
            else:
                out[d, 0, :, cols(1, c)] = rs_sum(1, d, c, xin[d, :, cols(1, c)])

    experts(0, 0)
    ag_hop(1, 1, 2)
    ag_hop(1, 0, 4)
    experts(0, 1)
    ag_hop(1, 1, 3)
    all_down(0)
    hop_all(0, 0)
    experts(1, 0)
    ag_hop(1, 1, 4)
    hop_all(0, 1)
    experts(1, 1)
    hop_all(0, 2)
    all_down(1)
    hop_all(1, 0)
    hop_all(0, 3)
    hop_all(1, 1)
    hop_all(0, 4)
    for h in range(2, 5):
        hop_all(1, h)

    for c in range(NC[0]):
        for h in range(4):
            for copy in rs_copies(0, 0, c, h) + rs_copies(0, 1, c, h):
                copy.wait_send()
        for copy in (shift(0, c), shift(1, c)) + wd_own(c) + wd_on(c):
            copy.wait_send()
    for d in range(2):
        for c in range(NC[1]):
            for h in range(4):
                for copy in rs_copies(1, d, c, h):
                    copy.wait_send()
    for copy in sent:
        copy.wait_send()


def solution(mesh):
    n_section = mesh.shape["section"]

    def per_device(state, fresh, norm_gain, w_gate, w_up, w_down, routes, gates):
        vmem = pl.BlockSpec(memory_space=pltpu.VMEM)
        hbm = pl.BlockSpec(memory_space=pl.ANY)
        return pl.pallas_call(
            functools.partial(kernel, n_section),
            out_shape=jax.ShapeDtypeStruct(state.shape, state.dtype),
            in_specs=[vmem, vmem, vmem, hbm, hbm, hbm, vmem, vmem],
            out_specs=vmem,
            scratch_shapes=[
                pltpu.VMEM((NX, D, 2 * HID), BF16),
                pltpu.VMEM((NX * HID, D), BF16),
                pltpu.VMEM((2, 2, NY * ROWS, D), BF16),
                pltpu.VMEM((2, NY * ROWS, NX * HID), BF16),
                pltpu.VMEM((2, NY * ROWS, D), F32),
                pltpu.VMEM((2, 2, 4, 2, ROWS, D), BF16),
                pltpu.VMEM((2, 2, ROWS, D), BF16),
                pltpu.VMEM((2, ROWS, D), BF16),
                pltpu.VMEM((2, ROWS, D), BF16),
                pltpu.VMEM((NY, 4 * ROWS, 128), F32),
                pltpu.SemaphoreType.DMA((N_SEMS,)),
                pltpu.SemaphoreType.DMA((N_SEMS,)),
                pltpu.SemaphoreType.DMA((3,)),
            ],
            compiler_params=pltpu.CompilerParams(
                collective_id=0, has_side_effects=True, vmem_limit_bytes=58 * 2**20),
        )(state, fresh, norm_gain, w_gate, w_up, w_down, jnp.swapaxes(routes, 3, 4), jnp.swapaxes(gates, 3, 4))

    rows = P(None, "section", "expert", None)
    named = P(None, None, "section", "expert", None)
    return jax.shard_map(
        per_device, mesh=mesh,
        in_specs=(rows, P(None, "expert", None), P("section", None), P("section", None, "expert"),
                  P("section", None, "expert"), P("section", "expert", None), named, named),
        out_specs=rows, check_vma=False)
```

```python
import functools

import jax
import jax.numpy as jnp
from jax import lax
from jax.experimental import pallas as pl
from jax.experimental.pallas import tpu as pltpu
from jax.sharding import PartitionSpec as P

MESH = pl.DeviceIdType.MESH
NX, NY = 4, 8
ROWS = 32
HALF = ROWS // 2
D = 3584
HID = 128
NC = (7, 4)
COLS = (D // NC[0], D // NC[1])
QROWS = D // 2
N_SEMS = 320
F32, BF16 = jnp.float32, jnp.bfloat16


def kernel(n_section, state, fresh, gain, w_gate, w_up, w_down, routes, gates, out,
           wgu, wd, xn, hid, part, rsb, snd, xs, xin, cw, send_sem, recv_sem, local_sem):
    expert = lax.axis_index("expert")
    section = lax.axis_index("section")
    ix, iy = expert // NY, expert % NY

    def along(dx, dy):
        return {"expert": ((ix + dx + NX) % NX) * NY + (iy + dy + NY) % NY}

    right, left = along(0, 1), along(0, -1)
    x_right, x_left = along(1, 0), along(-1, 0)
    onward = {"section": (section + 1) % n_section}
    backward = {"section": (section + n_section - 1) % n_section}

    count = [0]
    sent = []

    def reserve(n):
        count[0] += n
        return count[0] - n

    def copy_to(src, dst, device, at=None):
        keep = at is None
        if keep:
            at = reserve(1)
        copy = pltpu.make_async_remote_copy(
            src_ref=src, dst_ref=dst, send_sem=send_sem.at[at], recv_sem=recv_sem.at[at],
            device_id=device, device_id_type=MESH)
        if keep:
            sent.append(copy)
        return copy

    barrier = pltpu.get_barrier_semaphore()
    for peer in (right, left, x_right, x_left, onward, backward):
        pl.semaphore_signal(barrier, inc=1, device_id=peer, device_id_type=MESH)

    own = [
        pltpu.make_async_copy(w_gate.at[0], wgu.at[0, :, pl.ds(0, HID)], local_sem.at[0]),
        pltpu.make_async_copy(w_up.at[0], wgu.at[0, :, pl.ds(HID, HID)], local_sem.at[1]),
        pltpu.make_async_copy(w_down.at[0], wd.at[pl.ds(0, HID)], local_sem.at[2])]

    def normed(x):
        wide = x.astype(F32)
        mean_sq = jnp.mean(wide * wide, axis=-1, keepdims=True)
        return (wide * lax.rsqrt(mean_sq + 1e-06) * gain[...]).astype(BF16)

    def slot(s, half=None):
        if half is None:
            return pl.ds(s * ROWS, ROWS)
        return pl.ds(s * ROWS + half * HALF, HALF)

    def q_rows(q):
        return pl.ds(q * QROWS, QROWS)

    def gu_own(q, r, device):
        return [copy_to(w.at[0, q_rows(q)], wgu.at[r, q_rows(q), pl.ds(k * HID, HID)], device)
                for k, w in enumerate((w_gate, w_up))]

    gu_r = [gu_own(q, 1, x_right) for q in range(2)]
    gu_l = [gu_own(q, 3, x_left) for q in range(2)]
    gu_fr = copy_to(wgu.at[1, q_rows(0)], wgu.at[2, q_rows(0)], x_right)
    gu_fl = copy_to(wgu.at[3, q_rows(1)], wgu.at[2, q_rows(1)], x_left)

    def cols(t, c):
        at = c * COLS[t]
        return pl.ds(at if isinstance(c, int) else pl.multiple_of(at, 128), COLS[t])

    def wd_at(r, c, half=None):
        if half is None:
            return wd.at[pl.ds(r * HID, HID), cols(0, c)]
        return wd.at[pl.ds(r * HID + half * (HID // 2), HID // 2), cols(0, c)]

    wd_sems = reserve(4 * NC[0])

    def wd_own(c):
        return (copy_to(w_down.at[0, :, cols(0, c)], wd_at(1, c), x_right, wd_sems + 4 * c),
                copy_to(w_down.at[0, :, cols(0, c)], wd_at(3, c), x_left, wd_sems + 4 * c + 1))

    def wd_on(c):
        return (copy_to(wd_at(1, c, 0), wd_at(2, c, 0), x_right, wd_sems + 4 * c + 2),
                copy_to(wd_at(3, c, 1), wd_at(2, c, 1), x_left, wd_sems + 4 * c + 3))

    def wd_pass(c):
        for came, on in zip(wd_own(c), wd_on(c)):
            came.wait_recv()
            on.start()

    def start(copies):
        for copy in copies:
            copy.start()

    def arrive(copies):
        for copy in copies:
            copy.wait_recv()

    def gather(t, d):
        ring = []
        for h in range(4):
            pieces = []
            for k in range(2):
                to_right = to_left = None
                if h < 3 or k == 0:
                    to_right = copy_to(xn.at[t, d, slot(h, k)], xn.at[t, d, slot(h + 1, k)], right)
                if h < 3 or k == 1:
                    to_left = copy_to(xn.at[t, d, slot((8 - h) % 8, k)], xn.at[t, d, slot(7 - h, k)], left)
                pieces.append((to_right, to_left))
            ring.append(pieces)
        return ring

    ag = [[gather(t, d) for d in range(2)] for t in range(2)]

    def ag_hop(t, d, h):
        for k in range(2):
            for side in range(2):
                if h > 0 and ag[t][d][h - 1][k][side] is not None:
                    ag[t][d][h - 1][k][side].wait_recv()
                if h < 4 and ag[t][d][h][k][side] is not None:
                    ag[t][d][h][k][side].start()

    cw_ring = [(copy_to(cw.at[h], cw.at[h + 1], right),
                copy_to(cw.at[(8 - h) % 8], cw.at[7 - h], left) if h < 3 else None) for h in range(4)]

    def cw_hop(h):
        for side in range(2):
            if h > 0 and cw_ring[h - 1][side] is not None:
                cw_ring[h - 1][side].wait_recv()
            if h < 4 and cw_ring[h][side] is not None:
                cw_ring[h][side].start()

    def combine_weights():
        column_expert = ((ix + NX - lax.broadcasted_iota(jnp.int32, (ROWS, 128), 1) % NX) % NX).astype(F32)
        eye = (lax.broadcasted_iota(jnp.int32, (ROWS, ROWS), 0)
               == lax.broadcasted_iota(jnp.int32, (ROWS, ROWS), 1))

        def column(row):
            return jnp.sum(jnp.where(eye, row, 0.0), axis=1, keepdims=True)

        for t in range(2):
            for d in range(2):
                ids, wts = routes[t, d, 0].astype(F32), gates[t, d, 0]
                cw[0, pl.ds((t * 2 + d) * ROWS, ROWS)] = (
                    jnp.where(column(ids[0:1]) == column_expert, column(wts[0:1]), 0.0)
                    + jnp.where(column(ids[1:2]) == column_expert, column(wts[1:2]), 0.0))

    def gate_up(t, d, r, first=0, last=NY):
        rows = pl.ds(first * ROWS, (last - first) * ROWS)
        joined = jnp.dot(xn[t, d, rows], wgu[r], preferred_element_type=F32)
        g, u = joined[:, :HID], joined[:, HID:]
        own_rows = pl.ds(pl.multiple_of((t * 2 + d) * ROWS, ROWS), ROWS)
        weights = cw[first:last, own_rows, :].reshape((last - first) * ROWS, 128)
        lane = lax.broadcasted_iota(jnp.int32, weights.shape, 1)
        weight = jnp.sum(jnp.where(lane == r, weights, 0.0), axis=1, keepdims=True)
        hidden = g / (1.0 + jnp.exp(-g)) * u * weight
        hid[d, rows, pl.ds(pl.multiple_of(r * HID, HID), HID)] = hidden.astype(BF16)

    def down(d, at):
        part[d, :, at] = jnp.dot(hid[d], wd[:, at], preferred_element_type=F32)

    rs_sems = [reserve(16 * n) for n in NC]

    def rs_copies(t, d, c, h):
        at = rs_sems[t] + ((d * NC[t] + c) * 4 + h) * 2
        if h == 0:
            return [copy_to(snd.at[t, d, pl.ds(k * HALF, HALF), cols(t, c)],
                            rsb.at[t, k, 0, d, pl.ds(k * HALF, HALF), cols(t, c)], (right, left)[k], at + k)
                    for k in range(2)]
        return [copy_to(rsb.at[t, k, h - 1, d, :, cols(t, c)], rsb.at[t, k, h, d, :, cols(t, c)],
                        (right, left)[k], at + k) for k in range(2)]

    def rs_hop(t, d, c, h):
        at_cols, onto = cols(t, c), rs_copies(t, d, c, h)
        if h == 0:
            snd[t, d, :, at_cols] = part[d, slot(4), at_cols].astype(BF16)
            start(onto)
            return
        came = rs_copies(t, d, c, h - 1)
        for side in range(2):
            mine = (4 + h) if side == 0 else (4 - h)
            came[side].wait_recv()
            buf = rsb.at[t, side, h - 1, d]
            if h == 1:
                at, lone = pl.ds(side * HALF, HALF), pl.ds((1 - side) * HALF, HALF)
                buf[at, at_cols] = (buf[at, at_cols].astype(F32) + part[d, slot(mine, side), at_cols]).astype(BF16)
                buf[lone, at_cols] = part[d, slot(mine, 1 - side), at_cols].astype(BF16)
            else:
                buf[:, at_cols] = (buf[:, at_cols].astype(F32) + part[d, slot(mine), at_cols]).astype(BF16)
            onto[side].start()

    def rs_sum(t, d, c, x):
        at_cols = cols(t, c)
        arrive(rs_copies(t, d, c, 3))
        mixed = (part[d, slot(0), at_cols] + rsb[t, 0, 3, d, :, at_cols].astype(F32)
                 + rsb[t, 1, 3, d, :, at_cols].astype(F32))
        return (x.astype(F32) + mixed).astype(BF16)

    shift_sems = reserve(2 * NC[0])

    def shift(d, c):
        return copy_to(xs.at[d, :, cols(0, c)], xin.at[d, :, cols(0, c)], {"section": (
            section + n_section + 1 - 2 * d) % n_section}, shift_sems + d * NC[0] + c)

    def hand_on(d, c):
        xs[d, :, cols(0, c)] = rs_sum(0, d, c, state[d, 0, :, cols(0, c)])
        shift(d, c).start()

    def next_input(d):
        for c in range(NC[0]):
            shift(d, c).wait_recv()

        @pl.when(section == (0 if d == 0 else n_section - 1))
        def _():
            xin[d] = fresh[d]

        xn[1, d, slot(0)] = normed(xin[d])

    pl.semaphore_wait(barrier, 6)
    start(gu_r[0])
    start(gu_l[1])
    start(gu_r[1])
    start(gu_l[0])
    for copy in own:
        copy.start()
    xn[0, 0, slot(0)] = normed(state[0, 0])
    ag_hop(0, 0, 0)
    xn[0, 1, slot(0)] = normed(state[1, 0])
    ag_hop(0, 1, 0)
    combine_weights()
    cw_hop(0)
    ag_hop(0, 0, 1)
    ag_hop(0, 1, 1)
    cw_hop(1)
    arrive(gu_r[0])
    gu_fr.start()
    arrive(gu_l[1])
    gu_fl.start()
    ag_hop(0, 0, 2)
    ag_hop(0, 1, 2)
    for c in (0, 1):
        start(wd_own(c))
    cw_hop(2)
    ag_hop(0, 0, 3)
    ag_hop(0, 1, 3)
    cw_hop(3)
    ag_hop(0, 0, 4)
    ag_hop(0, 1, 4)
    cw_hop(4)
    for copy in own:
        copy.wait()
    arrive(gu_r[1])
    arrive(gu_l[0])

    @pl.loop(0, 6)
    def _(j):
        gate_up(0, j % 2, j // 2 + j // 4)

    gu_fr.wait_recv()
    gu_fl.wait_recv()

    @pl.loop(0, 2)
    def _(d):
        gate_up(0, d, 2)

    wd_pass(0)
    start(wd_own(2))
    wd_pass(1)
    start(wd_own(3))

    def back_hops(d, i):
        for h in (4, 3, 2, 1):
            if 0 <= i - h < NC[0]:
                if h == 4:
                    hand_on(d, i - h)
                else:
                    rs_hop(0, d, i - h, h)

    for i in range(NC[0] + 4):
        back_hops(0, i)
        if i < NC[0]:
            arrive(wd_on(i))

            @pl.loop(0, 2)
            def _(d):
                down(d, cols(0, i))

            rs_hop(0, 0, i, 0)
        if i + 2 < NC[0]:
            wd_pass(i + 2)
        if i + 4 < NC[0]:
            start(wd_own(i + 4))
        back_hops(1, i - 2)
        if 0 <= i - 2 < NC[0]:
            rs_hop(0, 1, i - 2, 0)

    back_hops(1, NC[0] + 2)
    next_input(0)
    ag_hop(1, 0, 0)
    back_hops(1, NC[0] + 3)
    ag_hop(1, 0, 1)
    next_input(1)
    ag_hop(1, 1, 0)
    ag_hop(1, 0, 2)
    ag_hop(1, 1, 1)
    ag_hop(1, 0, 3)

    def experts(d, half):
        @pl.loop(0, NX)
        def _(r):
            gate_up(1, d, r, half * NY // 2, (half + 1) * NY // 2)

    def all_down(d):
        @pl.loop(0, D // 512)
        def _(c):
            down(d, pl.ds(pl.multiple_of(c * 512, 512), 512))

    def hop_all(d, h):
        for c in range(NC[1]):
            if h < 4:
                rs_hop(1, d, c, h)
            else:
                out[d, 0, :, cols(1, c)] = rs_sum(1, d, c, xin[d, :, cols(1, c)])

    experts(0, 0)
    ag_hop(1, 1, 2)
    ag_hop(1, 0, 4)
    experts(0, 1)
    ag_hop(1, 1, 3)
    all_down(0)
    hop_all(0, 0)
    experts(1, 0)
    ag_hop(1, 1, 4)
    hop_all(0, 1)
    experts(1, 1)
    hop_all(0, 2)
    all_down(1)
    hop_all(1, 0)
    hop_all(0, 3)
    hop_all(1, 1)
    hop_all(0, 4)
    for h in range(2, 5):
        hop_all(1, h)

    for c in range(NC[0]):
        for h in range(4):
            for copy in rs_copies(0, 0, c, h) + rs_copies(0, 1, c, h):
                copy.wait_send()
        for copy in (shift(0, c), shift(1, c)) + wd_own(c) + wd_on(c):
            copy.wait_send()
    for d in range(2):
        for c in range(NC[1]):
            for h in range(4):
                for copy in rs_copies(1, d, c, h):
                    copy.wait_send()
    for copy in sent:
        copy.wait_send()


def solution(mesh):
    n_section = mesh.shape["section"]

    def per_device(state, fresh, norm_gain, w_gate, w_up, w_down, routes, gates):
        vmem = pl.BlockSpec(memory_space=pltpu.VMEM)
        hbm = pl.BlockSpec(memory_space=pl.ANY)
        return pl.pallas_call(
            functools.partial(kernel, n_section),
            out_shape=jax.ShapeDtypeStruct(state.shape, state.dtype),
            in_specs=[vmem, vmem, vmem, hbm, hbm, hbm, vmem, vmem],
            out_specs=vmem,
            scratch_shapes=[
                pltpu.VMEM((NX, D, 2 * HID), BF16),
                pltpu.VMEM((NX * HID, D), BF16),
                pltpu.VMEM((2, 2, NY * ROWS, D), BF16),
                pltpu.VMEM((2, NY * ROWS, NX * HID), BF16),
                pltpu.VMEM((2, NY * ROWS, D), F32),
                pltpu.VMEM((2, 2, 4, 2, ROWS, D), BF16),
                pltpu.VMEM((2, 2, ROWS, D), BF16),
                pltpu.VMEM((2, ROWS, D), BF16),
                pltpu.VMEM((2, ROWS, D), BF16),
                pltpu.VMEM((NY, 4 * ROWS, 128), F32),
                pltpu.SemaphoreType.DMA((N_SEMS,)),
                pltpu.SemaphoreType.DMA((N_SEMS,)),
                pltpu.SemaphoreType.DMA((3,)),
            ],
            compiler_params=pltpu.CompilerParams(
                collective_id=0, has_side_effects=True, vmem_limit_bytes=58 * 2**20),
        )(state, fresh, norm_gain, w_gate, w_up, w_down, jnp.swapaxes(routes, 3, 4), jnp.swapaxes(gates, 3, 4))

    rows = P(None, "section", "expert", None)
    named = P(None, None, "section", "expert", None)
    return jax.shard_map(
        per_device, mesh=mesh,
        in_specs=(rows, P(None, "expert", None), P("section", None), P("section", None, "expert"),
                  P("section", None, "expert"), P("section", "expert", None), named, named),
        out_specs=rows, check_vma=False)
```
